32 devices in a mesh: blk: 4 (over y, x), group: 8 (over z, core).
Axes of the slice: x: 2, y: 2, z: 4, core: 2. Of those that a mesh axis runs over, the one named last changes fastest.
Arguments:
- walk_rows: bfloat16 [2048, 32768], P('blk', 'group'), may hold values from -6 to 6
- col_values: bfloat16 [12288, 2048], P('group', 'blk'), may hold values from -0.0546875 to 0.0546875
- col_index: int32 [24, 4], P('group'), may hold values from 0 to 7
- col_count: int32 [8, 4], P('group'), may hold values from 1 to 3, as said below
Outputs:
- inflated: float32 [2048, 2048], P(('blk', 'group'))
The draws below stay inside these ranges and needn't reach their ends.
Inputs may be any that keep to these rules, and one draw needn't show every extreme that they name: `col_count`: each list holds 1 to 3 valid slots; some list holds 3; contents of the other slots are arbitrary.
All inputs are finite; a program needn't handle non-finite values.
Results may differ from the reference program's by a relative error of at most 0.0003.
Values may be sent and summed in bfloat16 or wider, within the bound.
A program may use at most 64 MiB of HBM per device.

```python
import jax
import jax.numpy as jnp
from jax import lax

BS = 512
KG = 8
LMAX = 3
ROWS = 2048
INNER = 32768
COLS = 2048
SLOTS = 24
N_BLK = 4
N_GROUP = 8


def draw_col_count(key, part):
    keys = jax.random.split(key, 3)
    heavy = jax.random.randint(keys[0], (N_GROUP, N_BLK), 0, 4) == 0
    counts = jnp.where(heavy, LMAX, 1)
    row = jax.random.randint(keys[1], (), 0, N_GROUP)
    column = jax.random.randint(keys[2], (), 0, N_BLK)
    counts = counts.at[row, column].set(LMAX)
    return counts.astype(jnp.int32)


def touch_ends(values, stream_key, low, top_value):
    shape = values.shape
    place = [jax.random.randint(jax.random.fold_in(stream_key, axis), (), 0, shape[axis]) for axis in range(len(shape))]
    values = values.at[tuple(place)].set(low)
    longest = shape.index(max(shape))
    place[longest] = (place[longest] + 1) % shape[longest]
    return values.at[tuple(place)].set(top_value)


def spiked(values, own_key, source, target, blocks, factor):
    def block_of(dim):
        return (jnp.arange(values.shape[dim]) // (values.shape[dim] // blocks)).reshape((-1,) + (1,) * (values.ndim - 1 - dim))

    near = jax.random.permutation(own_key, blocks)[block_of(target)]
    far = (block_of(target) + blocks // 2) % blocks
    return jnp.where((block_of(source) == near) | (block_of(source) == far), factor * values, values)


def steps_of(key, dims, shards, smallest, high):
    loudness, own = 1.0, jax.random.fold_in(key, 6)
    for dim, shards_of in shards:
        draws = jnp.exp(jax.random.uniform(jax.random.fold_in(own, dim), (shards_of,), jnp.float32, smallest / len(shards), high / len(shards)))
        loudness = loudness * jnp.repeat(draws, dims[dim] // shards_of).reshape([-1 if axis == dim else 1 for axis in range(len(dims))])
    return loudness


def centred(key, dims, deviation, most, cuts=(), held_as=jnp.bfloat16):
    array = jax.random.normal(key, dims, jnp.float32) * deviation
    if len(cuts) > 0:
        array = steps_of(key, dims, cuts, -0.22, 0.18) * array
    return jnp.clip(array, min=-most, max=most).astype(held_as)


def heavy_noise(stream_key, shape, deviation, most, shards, heavy, kind=jnp.bfloat16):
    drawn = deviation * jax.random.normal(stream_key, shape, jnp.float32)
    if shards:
        drawn = drawn * steps_of(stream_key, shape, shards, -0.22, 0.18)
    return jnp.clip(spiked(drawn, jax.random.fold_in(stream_key, 3), *heavy), -most, most).astype(kind)


def setup_inputs(seed: int = 0) -> dict:
    seeds = jax.random.split(jax.random.key(seed), 5)
    walk_rows = heavy_noise(seeds[0], (ROWS, INNER), 1.0, 6.0, ((0, 4), (1, 8)), (1, 0, 8, 2.0))
    col_values = centred(seeds[1], (SLOTS * BS, COLS), (BS * SLOTS) ** -0.5, 0.0546875, ((0, 8), (1, 4)))
    col_index = touch_ends(jax.random.randint(seeds[2], (SLOTS, N_BLK), 0, KG), jax.random.fold_in(seeds[2], 1), 0, KG - 1).astype(jnp.int32)
    col_count = draw_col_count(jax.random.fold_in(seeds[4], 71), 0)
    return dict(walk_rows=walk_rows, col_values=col_values, col_index=col_index, col_count=col_count)


def reference(walk_rows, col_values, col_index, col_count):
    def panel_product(panel):
        values = lax.dynamic_slice_in_dim(col_values, panel * BS, BS, 1)

        def group_step(total, group):
            for slot in range(LMAX):
                row = (group * LMAX + slot).astype(jnp.int32)
                inner = col_index[row, panel].astype(jnp.int32)
                start = ((group * KG + inner) * BS).astype(jnp.int32)
                block = lax.dynamic_slice_in_dim(walk_rows, start, BS, 1)
                piece = lax.dynamic_slice_in_dim(values, (row * BS).astype(jnp.int32), BS, 0)
                valid = slot < col_count[group, panel]
                product = jnp.dot(block, piece, preferred_element_type=jnp.float32)
                total = total + jnp.where(valid, product, jnp.zeros_like(product))
            return total, None

        total, unused = lax.scan(group_step, jnp.zeros((ROWS, BS), jnp.float32), jnp.arange(N_GROUP, dtype=jnp.int32))
        return total

    parts = lax.map(panel_product, jnp.arange(N_BLK, dtype=jnp.int32))
    expanded = jnp.transpose(parts, (1, 0, 2)).reshape(ROWS, COLS)
    squared = expanded * expanded
    scale = jnp.mean(squared, axis=0) + 1e-6
    return squared / scale
```

```python
import functools

import jax
import jax.numpy as jnp
from jax import lax
from jax.experimental import pallas as pl
from jax.experimental.pallas import tpu as pltpu
from jax.sharding import PartitionSpec as P

CHUNKS = 4
LAG = 3


def snake(i, n):
    half = n // 2
    return jnp.where(i < half, i, half + n - 1 - i)


def kernel(n, ng, a_hbm, b_hbm, idx_ref, cnt_ref, sq_ref, scale_ref,
           a_v, gath, part, sib, summed, zin, stat, stat2, gin, bin_,
           a_sem, b_sem, bs_sem, br_sem, xs_sem, xr_sem, zs_sem, zr_sem, s_sem):
    rows, width, nc = a_hbm.shape[0], b_hbm.shape[1], gath.shape[1]
    slots = b_hbm.shape[0] // width
    inner = a_hbm.shape[1] // width
    cw = width // nc
    share, nz = rows // ng, ng // 2
    units = n * nc
    me_b, me_g = lax.axis_index("blk"), lax.axis_index("group")
    core, z = me_g % 2, me_g // 2
    pos = snake(me_b, n)
    ring = (snake((pos + 1) % n, n), snake((pos + n - 1) % n, n))

    def b_copy(c):
        return pltpu.make_async_copy(
            b_hbm.at[:, pl.ds(pl.multiple_of(c * cw, cw), cw)], gath.at[me_b, c], b_sem.at[c])

    for c in range(nc):
        b_copy(c).start()
    for k in range(inner):
        pltpu.make_async_copy(a_hbm.at[:, k * width:(k + 1) * width], a_v.at[k], a_sem).start()

    barrier = pltpu.get_barrier_semaphore()

    @pl.loop(1, ng)
    def _(d):
        pl.semaphore_signal(barrier, inc=1, device_id={"group": (me_g + d) % ng},
                            device_id_type=pl.DeviceIdType.MESH)

    @pl.loop(1, n)
    def _(d):
        pl.semaphore_signal(barrier, inc=1, device_id={"blk": (me_b + d) % n},
                            device_id_type=pl.DeviceIdType.MESH)

    pl.semaphore_wait(barrier, ng - 1 + n - 1)

    def ring_copy(panel, c, d):
        to = ring[d] if isinstance(d, int) else jnp.where(d == 0, ring[0], ring[1])
        return pltpu.make_async_remote_copy(
            src_ref=gath.at[panel, c], dst_ref=gath.at[panel, c],
            send_sem=bs_sem.at[d, panel, c], recv_sem=br_sem.at[panel, c],
            device_id={"blk": to}, device_id_type=pl.DeviceIdType.MESH)

    def goes_on(hop, c, d):
        return (hop + 1 < n // 2) | ((hop + 1 == n // 2) & (c % 2 == d))

    def unit(t):
        u = t - nc
        own = t < nc
        hop = jnp.where(own, 0, 1 + u // (2 * nc))
        r = u % (2 * nc)
        c = jnp.where(own, t, jnp.where(hop == n // 2, r, r // 2))
        d = jnp.where(own, 0, r % 2)
        panel = snake((pos + jnp.where(d == 0, n - hop, hop)) % n, n)
        return hop, c, d, panel

    for c in range(nc):
        b_copy(c).wait()
        for d in range(2):
            if n // 2 > 1 or c % 2 == d:
                ring_copy(me_b, c, d).start()
    pltpu.make_async_copy(a_v, a_v, a_sem).wait()

    def sib_copy(t):
        return pltpu.make_async_remote_copy(
            src_ref=part.at[t, 1 - core], dst_ref=sib.at[t],
            send_sem=xs_sem.at[t], recv_sem=xr_sem.at[t],
            device_id={"group": me_g + 1 - 2 * core}, device_id_type=pl.DeviceIdType.MESH)

    def z_copy(t, d):
        to = (z + d) % nz
        return pltpu.make_async_remote_copy(
            src_ref=summed.at[t, to], dst_ref=zin.at[t, d - 1],
            send_sem=zs_sem.at[t], recv_sem=zr_sem.at[t],
            device_id={"group": to * 2 + core}, device_id_type=pl.DeviceIdType.MESH)

    def first(t):
        hop, c, d, panel = unit(t)

        @pl.when(hop > 0)
        def _():
            ring_copy(panel, c, d).wait_recv()

            @pl.when(goes_on(hop, c, d))
            def _():
                ring_copy(panel, c, d).start()

        total = jnp.zeros((rows, cw), jnp.float32)
        count = jnp.full((1, cw), cnt_ref[0, panel], jnp.int32)
        for s in range(slots):
            k = jnp.maximum(jnp.minimum(idx_ref[s, panel], inner - 1), 0)
            block = a_v[k]
            piece = gath[panel, c, s * width:(s + 1) * width, :]
            product = jnp.dot(block, piece, preferred_element_type=jnp.float32)
            total = total + jnp.where(s < count, product, 0.0)
        for q in range(ng):
            part[t, q % 2, q // 2] = total[q * share:(q + 1) * share]
        sib_copy(t).start()

    def second(t):
        sib_copy(t).wait_recv()
        summed[t] = part[t, core] + sib[t]

        @pl.loop(1, nz)
        def _(d):
            z_copy(t, d).start()

    def third(t):
        hop, c, d, panel = unit(t)
        pltpu.make_async_copy(zin.at[t], zin.at[t], zr_sem.at[t]).wait()
        total = summed[t, z]
        for i in range(nz - 1):
            total = total + zin[t, i]
        squared = total * total
        at = pl.ds(pl.multiple_of(panel * width + c * cw, cw), cw)
        sq_ref[:, at] = squared
        stat[:, at] = jnp.sum(squared, axis=0, keepdims=True)

    @pl.loop(0, units + LAG)
    def _(t):
        @pl.when(t < units)
        def _():
            first(t)

        @pl.when((t >= 1) & (t < units + 1))
        def _():
            second(t - 1)

        @pl.when(t >= LAG)
        def _():
            third(t - LAG)

    def exchange(source, into, axis, me, size, k):
        @pl.loop(1, size)
        def _(d):
            pltpu.make_async_remote_copy(
                src_ref=source, dst_ref=into.at[d - 1], send_sem=s_sem.at[k], recv_sem=s_sem.at[k + 1],
                device_id={axis: (me + d) % size}, device_id_type=pl.DeviceIdType.MESH).start()

        pltpu.make_async_copy(into, into, s_sem.at[k + 1]).wait()

    exchange(stat, gin, "group", me_g, ng, 0)
    stat2[...] = stat[...] + jnp.sum(gin[...], axis=0)
    exchange(stat2, bin_, "blk", me_b, n, 2)
    total = stat2[...] + jnp.sum(bin_[...], axis=0)
    scale_ref[...] = total / (n * rows) + 1e-6

    pltpu.make_async_copy(gin, gin, s_sem.at[0]).wait()
    pltpu.make_async_copy(bin_, bin_, s_sem.at[2]).wait()

    @pl.loop(0, units)
    def _(t):
        sib_copy(t).wait_send()
        pltpu.make_async_copy(zin.at[t], zin.at[t], zs_sem.at[t]).wait()
        hop, c, d, panel = unit(t)
        for way in range(2):
            @pl.when(((hop == 0) | (d == way)) & goes_on(hop, c, way))
            def _():
                ring_copy(panel, c, way).wait_send()


def on_device(walk_rows, col_values, col_index, col_count):
    n, ng = lax.axis_size("blk"), lax.axis_size("group")
    rows, width = walk_rows.shape[0], col_values.shape[1]
    cw, units, share, nz = width // CHUNKS, n * CHUNKS, rows // ng, ng // 2
    cols = n * width
    f32, bf16 = jnp.float32, jnp.bfloat16
    dma = pltpu.SemaphoreType.DMA
    squared, scale = pl.pallas_call(
        functools.partial(kernel, n, ng),
        out_shape=(jax.ShapeDtypeStruct((share, cols), f32), jax.ShapeDtypeStruct((1, cols), f32)),
        in_specs=[pl.BlockSpec(memory_space=pl.ANY)] * 2 + [pl.BlockSpec(memory_space=pltpu.SMEM)] * 2,
        out_specs=(pl.BlockSpec(memory_space=pltpu.VMEM),) * 2,
        scratch_shapes=[
            pltpu.VMEM((walk_rows.shape[1] // width, rows, width), bf16),
            pltpu.VMEM((n, CHUNKS, col_values.shape[0], cw), bf16),
            pltpu.VMEM((units, 2, nz, share, cw), f32),
            pltpu.VMEM((units, nz, share, cw), f32),
            pltpu.VMEM((units, nz, share, cw), f32),
            pltpu.VMEM((units, nz - 1, share, cw), f32),
            pltpu.VMEM((1, cols), f32),
            pltpu.VMEM((1, cols), f32),
            pltpu.VMEM((ng - 1, 1, cols), f32),
            pltpu.VMEM((n - 1, 1, cols), f32),
            dma, dma((CHUNKS,)), dma((2, n, CHUNKS)), dma((n, CHUNKS)),
            dma((units,)), dma((units,)), dma((units,)), dma((units,)), dma((4,)),
        ],
        compiler_params=pltpu.CompilerParams(
            collective_id=0, has_side_effects=True, vmem_limit_bytes=56 * 2**20),
    )(walk_rows, col_values, col_index, col_count)
    return squared / scale


def solution(mesh):
    return jax.shard_map(
        on_device,
        mesh=mesh,
        in_specs=(P("blk", "group"), P("group", "blk"), P("group", None), P("group", None)),
        out_specs=P(("blk", "group"), None),
        check_vma=False,
    )
```

```python
import functools

import jax
import jax.numpy as jnp
from jax import lax
from jax.experimental import pallas as pl
from jax.experimental.pallas import tpu as pltpu
from jax.sharding import PartitionSpec as P

CHUNKS = 4
LAG = 3


def snake(i, n):
    half = n // 2
    return jnp.where(i < half, i, half + n - 1 - i)


def kernel(n, ng, a_hbm, b_hbm, idx_ref, cnt_ref, sq_ref, scale_ref,
           a_v, gath, part, sib, summed, zin, stat, stat2, gin, bin_,
           a_sem, b_sem, bs_sem, br_sem, bh_sem, xs_sem, xr_sem, zs_sem, zr_sem, s_sem):
    rows, width, nc = a_hbm.shape[0], b_hbm.shape[1], gath.shape[1]
    slots = b_hbm.shape[0] // width
    inner = a_hbm.shape[1] // width
    cw = width // nc
    share, nz = rows // ng, ng // 2
    units = n * nc
    me_b, me_g = lax.axis_index("blk"), lax.axis_index("group")
    core, z = me_g % 2, me_g // 2
    pos = snake(me_b, n)
    ring = (snake((pos + 1) % n, n), snake((pos + n - 1) % n, n))

    def b_copy(c):
        return pltpu.make_async_copy(
            b_hbm.at[:, pl.ds(pl.multiple_of(c * cw, cw), cw)], gath.at[me_b, c], b_sem.at[c])

    for c in range(nc):
        b_copy(c).start()
    for k in range(inner):
        pltpu.make_async_copy(a_hbm.at[:, k * width:(k + 1) * width], a_v.at[k], a_sem).start()

    barrier = pltpu.get_barrier_semaphore()

    @pl.loop(1, ng)
    def _(d):
        pl.semaphore_signal(barrier, inc=1, device_id={"group": (me_g + d) % ng},
                            device_id_type=pl.DeviceIdType.MESH)

    @pl.loop(1, n)
    def _(d):
        pl.semaphore_signal(barrier, inc=1, device_id={"blk": (me_b + d) % n},
                            device_id_type=pl.DeviceIdType.MESH)

    pl.semaphore_wait(barrier, ng - 1 + n - 1)

    def ring_copy(panel, c, d):
        to = ring[d] if isinstance(d, int) else jnp.where(d == 0, ring[0], ring[1])
        return pltpu.make_async_remote_copy(
            src_ref=gath.at[panel, c], dst_ref=gath.at[panel, c],
            send_sem=bs_sem.at[d, panel, c], recv_sem=br_sem.at[panel, c],
            device_id={"blk": to}, device_id_type=pl.DeviceIdType.MESH)

    tall = slots * width // 2

    def half_copy(panel, c, d):
        part_of = gath.at[panel, c, pl.ds(pl.multiple_of(d * tall, tall), tall)]
        return pltpu.make_async_remote_copy(
            src_ref=part_of, dst_ref=part_of,
            send_sem=bs_sem.at[d, panel, c], recv_sem=bh_sem.at[d, c],
            device_id={"blk": ring[d] if isinstance(d, int) else jnp.where(d == 0, ring[0], ring[1])},
            device_id_type=pl.DeviceIdType.MESH)

    def pass_on(panel, hop, c, d, act):
        @pl.when(hop + 1 < n // 2)
        def _():
            act(ring_copy(panel, c, d))

        @pl.when(hop + 1 == n // 2)
        def _():
            act(half_copy(panel, c, d))

    def unit(t):
        u = t - nc
        own = t < nc
        hop = jnp.where(own, 0, 1 + u // (2 * nc))
        r = u % (2 * nc)
        c = jnp.where(own, t, jnp.where(hop == n // 2, r, r // 2))
        d = jnp.where(own, 0, r % 2)
        panel = snake((pos + jnp.where(d == 0, n - hop, hop)) % n, n)
        return hop, c, d, panel

    for c in range(nc):
        b_copy(c).wait()
        for d in range(2):
            pass_on(me_b, 0, c, d, lambda copy: copy.start())
    pltpu.make_async_copy(a_v, a_v, a_sem).wait()

    def sib_copy(t):
        return pltpu.make_async_remote_copy(
            src_ref=part.at[t, 1 - core], dst_ref=sib.at[t],
            send_sem=xs_sem.at[t], recv_sem=xr_sem.at[t],
            device_id={"group": me_g + 1 - 2 * core}, device_id_type=pl.DeviceIdType.MESH)

    def z_copy(t, d):
        to = (z + d) % nz
        return pltpu.make_async_remote_copy(
            src_ref=summed.at[t, to], dst_ref=zin.at[t, d - 1],
            send_sem=zs_sem.at[t], recv_sem=zr_sem.at[t],
            device_id={"group": to * 2 + core}, device_id_type=pl.DeviceIdType.MESH)

    def first(t):
        hop, c, d, panel = unit(t)

        @pl.when((hop > 0) & (hop < n // 2))
        def _():
            ring_copy(panel, c, d).wait_recv()
            pass_on(panel, hop, c, d, lambda copy: copy.start())

        @pl.when(hop == n // 2)
        def _():
            half_copy(panel, c, 0).wait_recv()
            half_copy(panel, c, 1).wait_recv()

        total = jnp.zeros((rows, cw), jnp.float32)
        count = jnp.full((1, cw), cnt_ref[0, panel], jnp.int32)
        for s in range(slots):
            k = jnp.maximum(jnp.minimum(idx_ref[s, panel], inner - 1), 0)
            block = a_v[k]
            piece = gath[panel, c, s * width:(s + 1) * width, :]
            product = jnp.dot(block, piece, preferred_element_type=jnp.float32)
            total = total + jnp.where(s < count, product, 0.0)
        for q in range(ng):
            part[t, q % 2, q // 2] = total[q * share:(q + 1) * share]
        sib_copy(t).start()

    def second(t):
        sib_copy(t).wait_recv()
        summed[t] = part[t, core] + sib[t]

        @pl.loop(1, nz)
        def _(d):
            z_copy(t, d).start()

    def third(t):
        hop, c, d, panel = unit(t)
        pltpu.make_async_copy(zin.at[t], zin.at[t], zr_sem.at[t]).wait()
        total = summed[t, z]
        for i in range(nz - 1):
            total = total + zin[t, i]
        squared = total * total
        at = pl.ds(pl.multiple_of(panel * width + c * cw, cw), cw)
        sq_ref[:, at] = squared
        stat[:, at] = jnp.sum(squared, axis=0, keepdims=True)

    @pl.loop(0, units + LAG)
    def _(t):
        @pl.when(t < units)
        def _():
            first(t)

        @pl.when((t >= 1) & (t < units + 1))
        def _():
            second(t - 1)

        @pl.when(t >= LAG)
        def _():
            third(t - LAG)

    def exchange(source, into, axis, me, size, k):
        @pl.loop(1, size)
        def _(d):
            pltpu.make_async_remote_copy(
                src_ref=source, dst_ref=into.at[d - 1], send_sem=s_sem.at[k], recv_sem=s_sem.at[k + 1],
                device_id={axis: (me + d) % size}, device_id_type=pl.DeviceIdType.MESH).start()

        pltpu.make_async_copy(into, into, s_sem.at[k + 1]).wait()

    exchange(stat, gin, "group", me_g, ng, 0)
    stat2[...] = stat[...] + jnp.sum(gin[...], axis=0)
    exchange(stat2, bin_, "blk", me_b, n, 2)
    total = stat2[...] + jnp.sum(bin_[...], axis=0)
    scale_ref[...] = total / (n * rows) + 1e-6

    pltpu.make_async_copy(gin, gin, s_sem.at[0]).wait()
    pltpu.make_async_copy(bin_, bin_, s_sem.at[2]).wait()

    @pl.loop(0, units)
    def _(t):
        sib_copy(t).wait_send()
        pltpu.make_async_copy(zin.at[t], zin.at[t], zs_sem.at[t]).wait()
        hop, c, d, panel = unit(t)
        for way in range(2):
            @pl.when((hop == 0) | (d == way))
            def _():
                pass_on(panel, hop, c, way, lambda copy: copy.wait_send())


def on_device(walk_rows, col_values, col_index, col_count):
    n, ng = lax.axis_size("blk"), lax.axis_size("group")
    rows, width = walk_rows.shape[0], col_values.shape[1]
    cw, units, share, nz = width // CHUNKS, n * CHUNKS, rows // ng, ng // 2
    cols = n * width
    f32, bf16 = jnp.float32, jnp.bfloat16
    dma = pltpu.SemaphoreType.DMA
    squared, scale = pl.pallas_call(
        functools.partial(kernel, n, ng),
        out_shape=(jax.ShapeDtypeStruct((share, cols), f32), jax.ShapeDtypeStruct((1, cols), f32)),
        in_specs=[pl.BlockSpec(memory_space=pl.ANY)] * 2 + [pl.BlockSpec(memory_space=pltpu.SMEM)] * 2,
        out_specs=(pl.BlockSpec(memory_space=pltpu.VMEM),) * 2,
        scratch_shapes=[
            pltpu.VMEM((walk_rows.shape[1] // width, rows, width), bf16),
            pltpu.VMEM((n, CHUNKS, col_values.shape[0], cw), bf16),
            pltpu.VMEM((units, 2, nz, share, cw), f32),
            pltpu.VMEM((units, nz, share, cw), f32),
            pltpu.VMEM((units, nz, share, cw), f32),
            pltpu.VMEM((units, nz - 1, share, cw), f32),
            pltpu.VMEM((1, cols), f32),
            pltpu.VMEM((1, cols), f32),
            pltpu.VMEM((ng - 1, 1, cols), f32),
            pltpu.VMEM((n - 1, 1, cols), f32),
            dma, dma((CHUNKS,)), dma((2, n, CHUNKS)), dma((n, CHUNKS)), dma((2, CHUNKS)),
            dma((units,)), dma((units,)), dma((units,)), dma((units,)), dma((4,)),
        ],
        compiler_params=pltpu.CompilerParams(
            collective_id=0, has_side_effects=True, vmem_limit_bytes=56 * 2**20),
    )(walk_rows, col_values, col_index, col_count)
    return squared / scale


def solution(mesh):
    return jax.shard_map(
        on_device,
        mesh=mesh,
        in_specs=(P("blk", "group"), P("group", "blk"), P("group", None), P("group", None)),
        out_specs=P(("blk", "group"), None),
        check_vma=False,
    )
```

```python
import functools

import jax
import jax.numpy as jnp
from jax import lax
from jax.experimental import pallas as pl
from jax.experimental.pallas import tpu as pltpu
from jax.sharding import PartitionSpec as P

CHUNKS = 4
LAG = 3


def snake(i, n):
    half = n // 2
    return jnp.where(i < half, i, half + n - 1 - i)


def kernel(n, ng, a_hbm, b_hbm, idx_ref, cnt_ref, sq_ref, scale_ref,
           a_v, gath, part, sib, summed, zin, stat, stat2, gin, bin_,
           a_sem, b_sem, bs_sem, br_sem, bh_sem, xs_sem, xr_sem, zs_sem, zr_sem, s_sem):
    rows, width, nc = a_hbm.shape[0], b_hbm.shape[1], gath.shape[1]
    slots = b_hbm.shape[0] // width
    inner = a_hbm.shape[1] // width
    cw = width // nc
    share, nz = rows // ng, ng // 2
    units = n * nc
    me_b, me_g = lax.axis_index("blk"), lax.axis_index("group")
    core, z = me_g % 2, me_g // 2
    pos = snake(me_b, n)
    ring = (snake((pos + 1) % n, n), snake((pos + n - 1) % n, n))

    def b_copy(c):
        return pltpu.make_async_copy(
            b_hbm.at[:, pl.ds(pl.multiple_of(c * cw, cw), cw)], gath.at[me_b, c], b_sem.at[c])

    for c in range(nc):
        b_copy(c).start()
    for k in range(inner):
        pltpu.make_async_copy(a_hbm.at[:, k * width:(k + 1) * width], a_v.at[k], a_sem).start()

    barrier = pltpu.get_barrier_semaphore()

    @pl.loop(1, ng)
    def _(d):
        pl.semaphore_signal(barrier, inc=1, device_id={"group": (me_g + d) % ng},
                            device_id_type=pl.DeviceIdType.MESH)

    @pl.loop(1, n)
    def _(d):
        pl.semaphore_signal(barrier, inc=1, device_id={"blk": (me_b + d) % n},
                            device_id_type=pl.DeviceIdType.MESH)

    pl.semaphore_wait(barrier, ng - 1 + n - 1)

    def ring_copy(panel, c, d):
        to = ring[d] if isinstance(d, int) else jnp.where(d == 0, ring[0], ring[1])
        return pltpu.make_async_remote_copy(
            src_ref=gath.at[panel, c], dst_ref=gath.at[panel, c],
            send_sem=bs_sem.at[d, panel, c], recv_sem=br_sem.at[panel, c],
            device_id={"blk": to}, device_id_type=pl.DeviceIdType.MESH)

    tall = slots * width // 2

    def half_copy(panel, c, d):
        part_of = gath.at[panel, c, pl.ds(pl.multiple_of(d * tall, tall), tall)]
        return pltpu.make_async_remote_copy(
            src_ref=part_of, dst_ref=part_of,
            send_sem=bs_sem.at[d, panel, c], recv_sem=bh_sem.at[d, c],
            device_id={"blk": ring[d] if isinstance(d, int) else jnp.where(d == 0, ring[0], ring[1])},
            device_id_type=pl.DeviceIdType.MESH)

    def pass_on(panel, hop, c, d, act):
        @pl.when(hop + 1 < n // 2)
        def _():
            act(ring_copy(panel, c, d))

        @pl.when(hop + 1 == n // 2)
        def _():
            act(half_copy(panel, c, d))

    def unit(t):
        u = t - nc
        own = t < nc
        hop = jnp.where(own, 0, 1 + u // (2 * nc))
        r = u % (2 * nc)
        c = jnp.where(own, t, jnp.where(hop == n // 2, r, r // 2))
        d = jnp.where(own, 0, r % 2)
        panel = snake((pos + jnp.where(d == 0, n - hop, hop)) % n, n)
        return hop, c, d, panel

    for c in range(nc):
        b_copy(c).wait()
        for d in range(2):
            pass_on(me_b, 0, c, d, lambda copy: copy.start())
    pltpu.make_async_copy(a_v, a_v, a_sem).wait()

    def sib_copy(t):
        return pltpu.make_async_remote_copy(
            src_ref=part.at[t, 1 - core], dst_ref=sib.at[t],
            send_sem=xs_sem.at[t], recv_sem=xr_sem.at[t],
            device_id={"group": me_g + 1 - 2 * core}, device_id_type=pl.DeviceIdType.MESH)

    def z_copy(t, d):
        to = (z + d) % nz
        return pltpu.make_async_remote_copy(
            src_ref=summed.at[t, to], dst_ref=zin.at[t, d - 1],
            send_sem=zs_sem.at[t], recv_sem=zr_sem.at[t],
            device_id={"group": to * 2 + core}, device_id_type=pl.DeviceIdType.MESH)

    def first(t):
        hop, c, d, panel = unit(t)

        @pl.when((hop > 0) & (hop < n // 2))
        def _():
            ring_copy(panel, c, d).wait_recv()
            pass_on(panel, hop, c, d, lambda copy: copy.start())

        @pl.when(hop == n // 2)
        def _():
            half_copy(panel, c, 0).wait_recv()
            half_copy(panel, c, 1).wait_recv()

        total = jnp.zeros((rows, cw), jnp.float32)
        count = jnp.full((1, cw), cnt_ref[0, panel], jnp.int32)
        for s in range(slots):
            k = jnp.maximum(jnp.minimum(idx_ref[s, panel], inner - 1), 0)
            block = a_v[k]
            piece = gath[panel, c, s * width:(s + 1) * width, :]
            product = jnp.dot(block, piece, preferred_element_type=jnp.float32)
            total = total + jnp.where(s < count, product, 0.0)
        for q in range(ng):
            part[t, q % 2, q // 2] = total[q * share:(q + 1) * share]
        sib_copy(t).start()

    def second(t):
        sib_copy(t).wait_recv()
        summed[t] = part[t, core] + sib[t]

        @pl.loop(1, nz)
        def _(d):
            z_copy(t, d).start()

    def third(t):
        hop, c, d, panel = unit(t)
        pltpu.make_async_copy(zin.at[t], zin.at[t], zr_sem.at[t]).wait()
        total = summed[t, z]
        for i in range(nz - 1):
            total = total + zin[t, i]
        squared = total * total
        at = pl.ds(pl.multiple_of(panel * width + c * cw, cw), cw)
        sq_ref[:, at] = squared
        stat[:, at] = jnp.sum(squared, axis=0, keepdims=True)

    @pl.loop(0, units + LAG)
    def _(t):
        @pl.when(t < units)
        def _():
            first(t)

        @pl.when((t >= 1) & (t < units - nc + 1))
        def _():
            second(t - 1)

        @pl.when((t >= units - nc) & (t < units))
        def _():
            second(t)

        @pl.when(t >= LAG)
        def _():
            third(t - LAG)

    def exchange(source, into, axis, me, size, k):
        @pl.loop(1, size)
        def _(d):
            pltpu.make_async_remote_copy(
                src_ref=source, dst_ref=into.at[d - 1], send_sem=s_sem.at[k], recv_sem=s_sem.at[k + 1],
                device_id={axis: (me + d) % size}, device_id_type=pl.DeviceIdType.MESH).start()

        pltpu.make_async_copy(into, into, s_sem.at[k + 1]).wait()

    exchange(stat, gin, "group", me_g, ng, 0)
    stat2[...] = stat[...] + jnp.sum(gin[...], axis=0)
    exchange(stat2, bin_, "blk", me_b, n, 2)
    total = stat2[...] + jnp.sum(bin_[...], axis=0)
    scale_ref[...] = total / (n * rows) + 1e-6

    pltpu.make_async_copy(gin, gin, s_sem.at[0]).wait()
    pltpu.make_async_copy(bin_, bin_, s_sem.at[2]).wait()

    @pl.loop(0, units)
    def _(t):
        sib_copy(t).wait_send()
        pltpu.make_async_copy(zin.at[t], zin.at[t], zs_sem.at[t]).wait()
        hop, c, d, panel = unit(t)
        for way in range(2):
            @pl.when((hop == 0) | (d == way))
            def _():
                pass_on(panel, hop, c, way, lambda copy: copy.wait_send())


def on_device(walk_rows, col_values, col_index, col_count):
    n, ng = lax.axis_size("blk"), lax.axis_size("group")
    rows, width = walk_rows.shape[0], col_values.shape[1]
    cw, units, share, nz = width // CHUNKS, n * CHUNKS, rows // ng, ng // 2
    cols = n * width
    f32, bf16 = jnp.float32, jnp.bfloat16
    dma = pltpu.SemaphoreType.DMA
    squared, scale = pl.pallas_call(
        functools.partial(kernel, n, ng),
        out_shape=(jax.ShapeDtypeStruct((share, cols), f32), jax.ShapeDtypeStruct((1, cols), f32)),
        in_specs=[pl.BlockSpec(memory_space=pl.ANY)] * 2 + [pl.BlockSpec(memory_space=pltpu.SMEM)] * 2,
        out_specs=(pl.BlockSpec(memory_space=pltpu.VMEM),) * 2,
        scratch_shapes=[
            pltpu.VMEM((walk_rows.shape[1] // width, rows, width), bf16),
            pltpu.VMEM((n, CHUNKS, col_values.shape[0], cw), bf16),
            pltpu.VMEM((units, 2, nz, share, cw), f32),
            pltpu.VMEM((units, nz, share, cw), f32),
            pltpu.VMEM((units, nz, share, cw), f32),
            pltpu.VMEM((units, nz - 1, share, cw), f32),
            pltpu.VMEM((1, cols), f32),
            pltpu.VMEM((1, cols), f32),
            pltpu.VMEM((ng - 1, 1, cols), f32),
            pltpu.VMEM((n - 1, 1, cols), f32),
            dma, dma((CHUNKS,)), dma((2, n, CHUNKS)), dma((n, CHUNKS)), dma((2, CHUNKS)),
            dma((units,)), dma((units,)), dma((units,)), dma((units,)), dma((4,)),
        ],
        compiler_params=pltpu.CompilerParams(
            collective_id=0, has_side_effects=True, vmem_limit_bytes=56 * 2**20),
    )(walk_rows, col_values, col_index, col_count)
    return squared / scale


def solution(mesh):
    return jax.shard_map(
        on_device,
        mesh=mesh,
        in_specs=(P("blk", "group"), P("group", "blk"), P("group", None), P("group", None)),
        out_specs=P(("blk", "group"), None),
        check_vma=False,
    )
```
